32 devices in a mesh: event: 4 (over z), blk: 8 (over y, x, core).
Axes of the slice: x: 2, y: 2, z: 4, core: 2. Of those that a mesh axis runs over, the one named last changes fastest.
Arguments:
- features: bfloat16 [4, 192, 64, 512], P('event', 'blk'), may hold values from -6 to 6
- occupancy: int32 [4, 192, 512], P('event', 'blk'), may hold values 0 or 1
- block_cells: int32 [4, 192], P('event'), may hold values from 0 to 63, as said below
- weight: bfloat16 [27, 64, 64], replicated, may hold values from -0.15625 to 0.15625
- cotangent: bfloat16 [4, 192, 64, 512], P('event', 'blk'), may hold values from -6 to 6
Outputs:
- output: bfloat16 [4, 192, 64, 512], P('event', 'blk')
- grad_features: bfloat16 [4, 192, 64, 512], P('event', 'blk')
- grad_weight: float32 [27, 64, 64], replicated
The draws below stay inside these ranges and needn't reach their ends.
Inputs may be any that keep to these rules, and one draw needn't show every extreme that they name: `block_cells`: blocks of an event are listed plane by plane, 24 to a plane, planes 0 to 7 in order; within a plane the cells are distinct and increasing. Index i of blk owns plane i.
All inputs are finite; a program needn't handle non-finite values. No bound on the sum of `occupancy` on one device may be relied on, other than what follows from the above.
Results may differ from the reference program's by a relative error of at most 0.001.
Values may be sent and summed in bfloat16 or wider, within the bound.
A program may use at most 128 MiB of HBM per device.

```python
import math
import jax
import jax.numpy as jnp
from jax import lax

CHANNELS = 64
EDGE = 8
VOXELS = 512
TAPS = 27
GRID_Y = 8
GRID_Z = 8
CELLS = 64
ACTIVE = 24
BLOCKS = 192
EVENTS = 4


def draw_block_cells(key, part):
    plane_total = EVENTS * BLOCKS // ACTIVE
    scores = jax.random.randint(key, (plane_total, CELLS), 0, 1 << 20) * CELLS + jnp.arange(CELLS, dtype=jnp.int32)[None, :]
    chosen = jnp.argsort(scores, axis=1)[:, :ACTIVE]
    return jnp.sort(chosen, axis=1).reshape(EVENTS, BLOCKS).astype(jnp.int32)


def with_ends(values, key, smallest, largest):
    extent = values.shape
    spot = [jax.random.randint(jax.random.fold_in(key, axis), (), 0, extent[axis]) for axis in range(len(extent))]
    values = values.at[tuple(spot)].set(smallest)
    longest = extent.index(max(extent))
    spot[longest] = (spot[longest] + 1) % extent[longest]
    return values.at[tuple(spot)].set(largest)


def shard_levels(own_key, dims, cuts, least, largest):
    gain, own = 1.0, jax.random.fold_in(own_key, 6)
    for axis_at, shards_of in cuts:
        steps = jnp.exp(jax.random.uniform(jax.random.fold_in(own, axis_at), (shards_of,), jnp.float32, least / len(cuts), largest / len(cuts)))
        gain = gain * jnp.repeat(steps, dims[axis_at] // shards_of).reshape([-1 if axis == axis_at else 1 for axis in range(len(dims))])
    return gain


def scatter_about(own_key, extent, width, limit, cuts=(), held_as=jnp.bfloat16):
    gain = shard_levels(own_key, extent, cuts, -0.22, 0.18) if cuts else 1.0
    array = jax.random.normal(own_key, extent, jnp.float32) * width * gain
    return jnp.minimum(jnp.maximum(array, -limit), limit).astype(held_as)


def setup_inputs(seed: int = 0) -> dict:
    splits = jax.random.split(jax.random.key(seed), 6)
    features = scatter_about(splits[0], (EVENTS, BLOCKS, CHANNELS, VOXELS), 1.0, 6.0, ((0, 4), (1, 8)))
    occupancy = with_ends((jax.random.randint(splits[1], (EVENTS, BLOCKS, VOXELS), 0, 2) < 1).astype(jnp.int32), jax.random.fold_in(splits[1], 1), 0, 1)
    block_cells = draw_block_cells(jax.random.fold_in(splits[5], 71), 0)
    weight = scatter_about(splits[3], (TAPS, CHANNELS, CHANNELS), (TAPS * CHANNELS) ** -0.5, 0.15625)
    cotangent = scatter_about(splits[4], (EVENTS, BLOCKS, CHANNELS, VOXELS), 1.0, 6.0, ((0, 4), (1, 8)))
    return {"features": features, "occupancy": occupancy, "block_cells": block_cells, "weight": weight, "cotangent": cotangent}


def offset_list():
    return [(step_x, step_y, step_z) for step_x in (-1, 0, 1) for step_y in (-1, 0, 1) for step_z in (-1, 0, 1)]


def ranges_for(offset_step):
    if offset_step < 0:
        return slice(0, 1), slice(EDGE - 1, EDGE)
    if offset_step > 0:
        return slice(EDGE + 1, EDGE + 2), slice(0, 1)
    return slice(1, EDGE + 1), slice(0, EDGE)


def neighbour_slots(own_plane, own_cells, table_gid, offset):
    row_y = own_cells // GRID_Z + offset[1]
    row_z = own_cells % GRID_Z + offset[2]
    inside = (row_y >= 0) & (row_y < GRID_Y) & (row_z >= 0) & (row_z < GRID_Z)
    target = (own_plane + offset[0]) * CELLS + row_y * GRID_Z + row_z
    matches = (target[:, None] == table_gid[None, :]) & inside[:, None]
    present = jnp.any(matches, axis=1)
    listing = jnp.arange(table_gid.shape[0], dtype=jnp.int32)[None, :]
    position = jnp.sum(jnp.where(matches, listing, 0), axis=1).astype(jnp.int32)
    return present, position


def build_padded(centre, table, own_plane, own_cells, table_gid):
    count = centre.shape[0]
    padded = jnp.zeros((count, CHANNELS, EDGE + 2, EDGE + 2, EDGE + 2), centre.dtype)
    padded = padded.at[:, :, 1:EDGE + 1, 1:EDGE + 1, 1:EDGE + 1].set(centre)
    for offset in offset_list():
        if offset == (0, 0, 0):
            continue
        present, position = neighbour_slots(own_plane, own_cells, table_gid, offset)
        dest_x, source_x = ranges_for(offset[0])
        dest_y, source_y = ranges_for(offset[1])
        dest_z, source_z = ranges_for(offset[2])
        slab = table[:, :, source_x, source_y, source_z]
        picked = jnp.take(slab, position, axis=0)
        picked = jnp.where(present[:, None, None, None, None], picked, jnp.zeros_like(picked))
        padded = padded.at[:, :, dest_x, dest_y, dest_z].set(picked)
    return padded


def columns(padded, orient):
    pieces = []
    for offset in offset_list():
        starts = [1 + orient * offset_step for offset_step in offset]
        piece = padded[:, :, starts[0]:starts[0] + EDGE, starts[1]:starts[1] + EDGE, starts[2]:starts[2] + EDGE]
        pieces.append(piece.reshape(padded.shape[0], CHANNELS, VOXELS))
    return jnp.concatenate(pieces, axis=1)


def reference(features, occupancy, block_cells, weight, cotangent):
    w_flat = weight.reshape(TAPS * CHANNELS, CHANNELS).astype(jnp.float32)
    w_back = jnp.transpose(weight, (1, 0, 2)).reshape(CHANNELS, TAPS * CHANNELS).astype(jnp.float32)
    group = math.gcd(BLOCKS, 4)
    group_count = BLOCKS // group

    def event_terms(operands):
        event_feat, event_occ, event_cells, event_cot = operands
        mask_half = event_occ.astype(jnp.bfloat16)
        masked = event_feat * mask_half[:, None, :]
        grad_masked = event_cot * mask_half[:, None, :]
        plane_ids = (jnp.arange(BLOCKS, dtype=jnp.int32) // ACTIVE).astype(jnp.int32)
        own_cells = event_cells.astype(jnp.int32)
        table_gid = plane_ids * CELLS + own_cells
        volume = masked.reshape(BLOCKS, CHANNELS, EDGE, EDGE, EDGE)
        grad_volume = grad_masked.reshape(BLOCKS, CHANNELS, EDGE, EDGE, EDGE)
        padded = build_padded(volume, volume, plane_ids, own_cells, table_gid)
        grad_padded = build_padded(grad_volume, grad_volume, plane_ids, own_cells, table_gid)
        shape_p = (group_count, group, CHANNELS, EDGE + 2, EDGE + 2, EDGE + 2)
        mask_full = event_occ.astype(jnp.float32).reshape(group_count, group, VOXELS)

        def group_terms(inner):
            padded_p, grad_padded_p, mask_p, grad_masked_p = inner
            col_x = columns(padded_p, 1).astype(jnp.float32)
            col_g = columns(grad_padded_p, -1).astype(jnp.float32)
            result = jnp.einsum('kc,bkv->bcv', w_flat, col_x, precision=lax.Precision.HIGHEST)
            out_p = (result * mask_p[:, None, :]).astype(jnp.bfloat16)
            grad_w = jnp.einsum('bkv,bcv->kc', col_x, grad_masked_p.astype(jnp.float32), precision=lax.Precision.HIGHEST)
            back = jnp.einsum('ik,bkv->biv', w_back, col_g, precision=lax.Precision.HIGHEST)
            grad_p = (back * mask_p[:, None, :]).astype(jnp.bfloat16)
            return out_p, grad_p, grad_w

        outs_p, grads_p, weights_p = lax.map(group_terms, (padded.reshape(shape_p), grad_padded.reshape(shape_p), mask_full, grad_masked.reshape(group_count, group, CHANNELS, VOXELS)))
        return outs_p.reshape(BLOCKS, CHANNELS, VOXELS), grads_p.reshape(BLOCKS, CHANNELS, VOXELS), jnp.sum(weights_p, axis=0)

    output, grad_features, grad_parts = lax.map(event_terms, (features, occupancy, block_cells, cotangent))
    grad_weight = jnp.sum(grad_parts, axis=0).reshape(TAPS, CHANNELS, CHANNELS)
    return output, grad_features, grad_weight
```

```python
import functools

import jax
import jax.numpy as jnp
from jax import lax
from jax.experimental import pallas as pl
from jax.experimental.pallas import tpu as pltpu
from jax.sharding import PartitionSpec as P

CHANNELS = 64
EDGE = 8
VOXELS = 512
FACE = EDGE * EDGE
TAPS = 27
GRID_Y = 8
GRID_Z = 8
ACTIVE = 24
PAIR = 2 * CHANNELS
HALF = TAPS // 2 + 1


def shifted(x, axis, by):
    devices = lax.axis_size(axis)
    pairs = [(i, i + by) for i in range(devices) if 0 <= i + by < devices]
    return lax.ppermute(x, axis, pairs)


def place(cell):
    return cell // GRID_Z * EDGE, pl.multiple_of(cell % GRID_Z * EDGE, EDGE)


def kernel(do_conv, do_gw, cells, x_ref, g_ref, occ_ref, lo_ref, hi_ref, *rest):
    rest = list(rest)
    w_ref = rest.pop(0) if do_conv else None
    out_ref, back_ref = (rest.pop(0), rest.pop(0)) if do_conv else (None, None)
    gw_ref = rest.pop(0) if do_gw else None
    plane, cols = rest[0], rest[1]
    rows_ref = rest[2] if do_gw else None

    def clear(i, _):
        plane[i] = jnp.zeros(plane.shape[1:], plane.dtype)
        return 0

    lax.fori_loop(0, EDGE + 2, clear, 0)
    if do_gw:
        gw_ref[...] = jnp.zeros(gw_ref.shape, gw_ref.dtype)

    def scatter(b, _):
        mask = occ_ref[pl.ds(b, 1), :].astype(jnp.float32)
        both = jnp.concatenate(
            [x_ref[b].astype(jnp.float32) * mask, g_ref[b].astype(jnp.float32) * mask], axis=0
        )
        if do_gw:
            rows_ref[b] = both.astype(jnp.bfloat16)
        y, z = place(cells[1, b])
        plane[1 : EDGE + 1, pl.ds(y + 1, EDGE), pl.ds(z + EDGE, EDGE), :] = both.T.reshape(
            EDGE, EDGE, EDGE, PAIR
        )
        y, z = place(cells[0, b])
        plane[0, pl.ds(y + 1, EDGE), pl.ds(z + EDGE, EDGE), :] = (
            lo_ref[b].astype(jnp.float32).reshape(EDGE, EDGE, PAIR)
        )
        y, z = place(cells[2, b])
        plane[EDGE + 1, pl.ds(y + 1, EDGE), pl.ds(z + EDGE, EDGE), :] = (
            hi_ref[b].astype(jnp.float32).reshape(EDGE, EDGE, PAIR)
        )
        return 0

    lax.fori_loop(0, ACTIVE, scatter, 0)

    def block(b, _):
        y, z = place(cells[1, b])
        for c in range(3):
            for e in range(3):
                part = plane[:, pl.ds(y + c, EDGE), pl.ds(z + EDGE - 1 + e, EDGE), :]
                at = (3 * c + e) * PAIR
                cols[:, at : at + PAIR] = part.reshape((EDGE + 2) * FACE, PAIR).astype(jnp.bfloat16)
        if do_gw:
            rows = rows_ref[b]
            gw_ref[:, : 5 * PAIR] += jnp.dot(
                rows, cols[FACE : FACE + VOXELS, 4 * PAIR :], preferred_element_type=jnp.float32
            )
            gw_ref[:, 5 * PAIR :] += jnp.dot(
                rows, cols[2 * FACE :, :], preferred_element_type=jnp.float32
            )
        if do_conv:
            total = jnp.dot(cols[:VOXELS, :], w_ref[0], preferred_element_type=jnp.float32)
            for a in (1, 2):
                total += jnp.dot(
                    cols[a * FACE : a * FACE + VOXELS, :],
                    w_ref[a],
                    preferred_element_type=jnp.float32,
                )
            mask = occ_ref[pl.ds(b, 1), :].astype(jnp.float32)
            result = (total.T * mask).astype(jnp.bfloat16)
            out_ref[b] = result[:CHANNELS]
            back_ref[b] = result[CHANNELS:]
        return 0

    lax.fori_loop(0, ACTIVE, block, 0)


def run(do_conv, do_gw, cells, x, g, occ, lo, hi, w):
    vmem = pl.BlockSpec(memory_space=pltpu.VMEM)
    operands = [cells, x, g, occ, lo, hi]
    shapes = []
    scratch = [
        pltpu.VMEM((EDGE + 2, GRID_Y * EDGE + 2, (GRID_Z + 2) * EDGE, PAIR), jnp.float32),
        pltpu.VMEM(((EDGE + 2) * FACE, 9 * PAIR), jnp.bfloat16),
    ]
    flops = 0
    if do_conv:
        operands.append(w)
        shapes += [jax.ShapeDtypeStruct(x.shape, x.dtype)] * 2
        flops += 4 * ACTIVE * VOXELS * TAPS * CHANNELS * PAIR * 2
    if do_gw:
        shapes.append(jax.ShapeDtypeStruct((PAIR, HALF * PAIR), jnp.float32))
        scratch.append(pltpu.VMEM((ACTIVE, PAIR, VOXELS), jnp.bfloat16))
        flops += 2 * ACTIVE * VOXELS * HALF * PAIR * PAIR * 2
    return pl.pallas_call(
        functools.partial(kernel, do_conv, do_gw),
        out_shape=shapes,
        in_specs=[pl.BlockSpec(memory_space=pltpu.SMEM)] + [vmem] * (len(operands) - 1),
        out_specs=[vmem] * len(shapes),
        scratch_shapes=scratch,
        cost_estimate=pl.CostEstimate(flops=flops, bytes_accessed=8 * x.size, transcendentals=0),
        compiler_params=pltpu.CompilerParams(vmem_limit_bytes=56 * 1024 * 1024),
    )(*operands)


def per_device(features, occupancy, block_cells, weight, cotangent):
    device = lax.axis_index("blk")
    x, g, occ = features[0], cotangent[0], occupancy[0]
    half = occ.astype(jnp.bfloat16)

    def faces(at):
        part = jnp.concatenate([x[:, :, at : at + FACE], g[:, :, at : at + FACE]], axis=1)
        part = part * half[:, None, at : at + FACE]
        return jnp.transpose(part, (0, 2, 1))

    from_below = shifted(faces(VOXELS - FACE), "blk", 1)
    from_above = shifted(faces(0), "blk", -1)
    filler = block_cells[0, :ACTIVE]
    listed = jnp.concatenate([filler, block_cells[0], filler])
    cells = lax.dynamic_slice_in_dim(listed, device * ACTIVE, 3 * ACTIVE).reshape(3, ACTIVE)
    none = jnp.zeros_like(weight)
    turned = jnp.transpose(weight[::-1], (0, 2, 1))
    w = jnp.concatenate(
        [jnp.concatenate([weight, none], axis=2), jnp.concatenate([none, turned], axis=2)], axis=1
    ).reshape(3, 9 * PAIR, PAIR)
    if SPLIT:
        (terms,) = run(False, True, cells, x, g, occ, from_below, from_above, w)
    else:
        output, back, terms = run(True, True, cells, x, g, occ, from_below, from_above, w)
    terms = terms.reshape(PAIR, HALF, PAIR)
    upper = jnp.transpose(terms[CHANNELS:, :, :CHANNELS], (1, 2, 0))
    lower = jnp.transpose(terms[:CHANNELS, :0:-1, CHANNELS:], (1, 0, 2))
    local = jnp.concatenate([lower, upper], axis=0).reshape(-1, PAIR)
    grad_weight = lax.psum(local, ("event", "blk")).reshape(TAPS, CHANNELS, CHANNELS)
    if SPLIT:
        output, back = run(True, False, cells, x, g, occ, from_below, from_above, w)
    return (output[None], back[None], grad_weight)


SPLIT = False


def solution(mesh):
    in_specs = (
        P("event", "blk", None, None),
        P("event", "blk", None),
        P("event", None),
        P(),
        P("event", "blk", None, None),
    )
    out_specs = (P("event", "blk", None, None), P("event", "blk", None, None), P())
    return jax.shard_map(
        per_device, mesh=mesh, in_specs=in_specs, out_specs=out_specs, check_vma=False
    )
```

```python
import functools

import jax
import jax.numpy as jnp
from jax import lax
from jax.experimental import pallas as pl
from jax.experimental.pallas import tpu as pltpu
from jax.sharding import PartitionSpec as P

CHANNELS = 64
EDGE = 8
VOXELS = 512
FACE = EDGE * EDGE
TAPS = 27
GRID_Y = 8
GRID_Z = 8
ACTIVE = 24
PAIR = 2 * CHANNELS
HALF = TAPS // 2 + 1


def shifted(x, axis, by):
    devices = lax.axis_size(axis)
    pairs = [(i, i + by) for i in range(devices) if 0 <= i + by < devices]
    return lax.ppermute(x, axis, pairs)


def place(cell):
    return cell // GRID_Z * EDGE, pl.multiple_of(cell % GRID_Z * EDGE, EDGE)


def turned(face):
    face = face.astype(jnp.float32)
    return jnp.concatenate([face[:, :FACE], face[:, FACE:]], axis=0).T


def kernel(do_conv, do_gw, cells, x_ref, g_ref, occ_ref, lo_ref, hi_ref, *rest):
    rest = list(rest)
    w_ref = rest.pop(0) if do_conv else None
    out_ref, back_ref = (rest.pop(0), rest.pop(0)) if do_conv else (None, None)
    gw_ref = rest.pop(0) if do_gw else None
    plane, cols = rest[0], rest[1]
    rows_ref = rest[2] if do_gw else None

    def clear(i, _):
        plane[i] = jnp.zeros(plane.shape[1:], plane.dtype)
        return 0

    lax.fori_loop(0, EDGE + 2, clear, 0)
    if do_conv:
        taps_ref = rest[-1]
        none = jnp.zeros((CHANNELS, CHANNELS), jnp.float32)
        for t in range(TAPS):
            a, at = t // 9, t % 9 * PAIR
            ahead = w_ref[t].astype(jnp.float32)
            behind = w_ref[TAPS - 1 - t].astype(jnp.float32).T
            taps_ref[a, at : at + CHANNELS] = jnp.concatenate([ahead, none], axis=1).astype(jnp.bfloat16)
            taps_ref[a, at + CHANNELS : at + PAIR] = jnp.concatenate([none, behind], axis=1).astype(
                jnp.bfloat16
            )
    if do_gw:
        sums = rest[3]
        sums[...] = jnp.zeros(sums.shape, sums.dtype)

    def scatter(b, _):
        mask = occ_ref[pl.ds(b, 1), :].astype(jnp.float32)
        both = jnp.concatenate(
            [x_ref[b].astype(jnp.float32) * mask, g_ref[b].astype(jnp.float32) * mask], axis=0
        )
        if do_gw:
            rows_ref[b] = both.astype(jnp.bfloat16)
        y, z = place(cells[1, b])
        plane[1 : EDGE + 1, pl.ds(y + 1, EDGE), pl.ds(z + EDGE, EDGE), :] = both.T.reshape(
            EDGE, EDGE, EDGE, PAIR
        )
        y, z = place(cells[0, b])
        plane[0, pl.ds(y + 1, EDGE), pl.ds(z + EDGE, EDGE), :] = (
            turned(lo_ref[b]).reshape(EDGE, EDGE, PAIR)
        )
        y, z = place(cells[2, b])
        plane[EDGE + 1, pl.ds(y + 1, EDGE), pl.ds(z + EDGE, EDGE), :] = (
            turned(hi_ref[b]).reshape(EDGE, EDGE, PAIR)
        )
        return 0

    lax.fori_loop(0, ACTIVE, scatter, 0)

    def block(b, _):
        y, z = place(cells[1, b])
        for c in range(3):
            for e in range(3):
                part = plane[:, pl.ds(y + c, EDGE), pl.ds(z + EDGE - 1 + e, EDGE), :]
                at = (3 * c + e) * PAIR
                cols[:, at : at + PAIR] = part.reshape((EDGE + 2) * FACE, PAIR).astype(jnp.bfloat16)
        if do_gw:
            rows = rows_ref[b]
            sums[:, : 5 * PAIR] += jnp.dot(
                rows, cols[FACE : FACE + VOXELS, 4 * PAIR :], preferred_element_type=jnp.float32
            )
            sums[:, 5 * PAIR :] += jnp.dot(
                rows, cols[2 * FACE :, :], preferred_element_type=jnp.float32
            )
        if do_conv:
            total = jnp.dot(cols[:VOXELS, :], taps_ref[0], preferred_element_type=jnp.float32)
            for a in (1, 2):
                total += jnp.dot(
                    cols[a * FACE : a * FACE + VOXELS, :],
                    taps_ref[a],
                    preferred_element_type=jnp.float32,
                )
            mask = occ_ref[pl.ds(b, 1), :].astype(jnp.float32)
            result = (total.T * mask).astype(jnp.bfloat16)
            out_ref[b] = result[:CHANNELS]
            back_ref[b] = result[CHANNELS:]
        return 0

    lax.fori_loop(0, ACTIVE, block, 0)
    if do_gw:
        for n in range(HALF):
            at = n * PAIR
            gw_ref[n] = jnp.concatenate(
                [
                    sums[CHANNELS:, at : at + PAIR].T[:CHANNELS],
                    sums[:CHANNELS, at + CHANNELS : at + PAIR],
                ],
                axis=1,
            )


def reduce_kernel(
    x_ref, o_ref, got, terms, whole, send_b, recv_b, send_e, recv_e, send_g, recv_g
):
    blk, event = lax.axis_index("blk"), lax.axis_index("event")
    blks, events = lax.axis_size("blk"), lax.axis_size("event")

    def near(k):
        return lax.rem(blk + k, blks)

    def far(k):
        return lax.rem(event + k, events)

    barrier = pltpu.get_barrier_semaphore()
    for k in range(1, blks):
        pl.semaphore_signal(
            barrier, inc=1, device_id=(event, near(k)), device_id_type=pl.DeviceIdType.MESH
        )
    for k in range(1, events):
        pl.semaphore_signal(
            barrier, inc=1, device_id=(far(k), blk), device_id_type=pl.DeviceIdType.MESH
        )
    pl.semaphore_wait(barrier, blks + events - 2)

    def send(src, dst, out_sem, in_sem, target):
        copy = pltpu.make_async_remote_copy(
            src_ref=src,
            dst_ref=dst,
            send_sem=out_sem,
            recv_sem=in_sem,
            device_id=target,
            device_id_type=pl.DeviceIdType.MESH,
        )
        copy.start()
        return copy

    copies = [
        send(x_ref.at[near(k)], got.at[k - 1], send_b.at[k], recv_b.at[k], (event, near(k)))
        for k in range(1, blks)
    ]
    total = x_ref[blk]
    for k, copy in enumerate(copies):
        copy.wait()
        total += got[k]
    terms[event] = total
    copies = [
        send(terms.at[event], terms.at[event], send_e.at[k], recv_e.at[k], (far(k), blk))
        for k in range(1, events)
    ]
    for copy in copies:
        copy.wait()
    total = terms[0]
    for k in range(1, events):
        total += terms[k]
    whole[blk] = total
    copies = [
        send(whole.at[blk], whole.at[blk], send_g.at[k], recv_g.at[k], (event, near(k)))
        for k in range(1, blks)
    ]
    for copy in copies:
        copy.wait()
    o_ref[...] = whole[...]


def reduced(local):
    blks, events = lax.axis_size("blk"), lax.axis_size("event")
    parts = local.reshape(blks, -1, PAIR)
    vmem = pl.BlockSpec(memory_space=pltpu.VMEM)
    sems = [pltpu.SemaphoreType.DMA((n,)) for n in (blks, blks, events, events, blks, blks)]
    total = pl.pallas_call(
        reduce_kernel,
        out_shape=jax.ShapeDtypeStruct(parts.shape, parts.dtype),
        in_specs=[vmem],
        out_specs=vmem,
        scratch_shapes=[
            pltpu.VMEM((blks - 1,) + parts.shape[1:], jnp.float32),
            pltpu.VMEM((events,) + parts.shape[1:], jnp.float32),
            pltpu.VMEM(parts.shape, jnp.float32),
        ]
        + sems,
        compiler_params=pltpu.CompilerParams(collective_id=0, has_side_effects=True),
    )(parts)
    return total.reshape(local.shape)


def run(do_conv, do_gw, cells, x, g, occ, lo, hi, w):
    vmem = pl.BlockSpec(memory_space=pltpu.VMEM)
    operands = [cells, x, g, occ, lo, hi]
    shapes = []
    scratch = [
        pltpu.VMEM((EDGE + 2, GRID_Y * EDGE + 2, (GRID_Z + 2) * EDGE, PAIR), jnp.float32),
        pltpu.VMEM(((EDGE + 2) * FACE, 9 * PAIR), jnp.bfloat16),
    ]
    flops = 0
    if do_conv:
        operands.append(w)
        shapes += [jax.ShapeDtypeStruct(x.shape, x.dtype)] * 2
        flops += 4 * ACTIVE * VOXELS * TAPS * CHANNELS * PAIR * 2
    if do_gw:
        shapes.append(jax.ShapeDtypeStruct((HALF, CHANNELS, PAIR), jnp.float32))
        scratch.append(pltpu.VMEM((ACTIVE, PAIR, VOXELS), jnp.bfloat16))
        scratch.append(pltpu.VMEM((PAIR, HALF * PAIR), jnp.float32))
        flops += 2 * ACTIVE * VOXELS * HALF * PAIR * PAIR * 2
    if do_conv:
        scratch.append(pltpu.VMEM((3, 9 * PAIR, PAIR), jnp.bfloat16))
    return pl.pallas_call(
        functools.partial(kernel, do_conv, do_gw),
        out_shape=shapes,
        in_specs=[pl.BlockSpec(memory_space=pltpu.SMEM)] + [vmem] * (len(operands) - 1),
        out_specs=[vmem] * len(shapes),
        scratch_shapes=scratch,
        cost_estimate=pl.CostEstimate(flops=flops, bytes_accessed=8 * x.size, transcendentals=0),
        compiler_params=pltpu.CompilerParams(vmem_limit_bytes=56 * 1024 * 1024),
    )(*operands)


def per_device(features, occupancy, block_cells, weight, cotangent):
    device = lax.axis_index("blk")
    x, g, occ = features[0], cotangent[0], occupancy[0]
    half = occ.astype(jnp.bfloat16)

    def faces(at):
        span = slice(at, at + FACE)
        mask = half[:, None, span]
        return jnp.concatenate([x[:, :, span] * mask, g[:, :, span] * mask], axis=2)

    from_below = shifted(faces(VOXELS - FACE), "blk", 1)
    from_above = shifted(faces(0), "blk", -1)
    filler = block_cells[0, :ACTIVE]
    listed = jnp.concatenate([filler, block_cells[0], filler])
    cells = lax.dynamic_slice_in_dim(listed, device * ACTIVE, 3 * ACTIVE).reshape(3, ACTIVE)
    w = weight
    if SPLIT:
        (terms,) = run(False, True, cells, x, g, occ, from_below, from_above, w)
    else:
        output, back, terms = run(True, True, cells, x, g, occ, from_below, from_above, w)
    terms = reduced(terms)
    grad_weight = jnp.concatenate([terms[:0:-1, :, CHANNELS:], terms[:, :, :CHANNELS]], axis=0)
    if SPLIT:
        output, back = run(True, False, cells, x, g, occ, from_below, from_above, w)
    return (output[None], back[None], grad_weight)


SPLIT = False


def solution(mesh):
    in_specs = (
        P("event", "blk", None, None),
        P("event", "blk", None),
        P("event", None),
        P(),
        P("event", "blk", None, None),
    )
    out_specs = (P("event", "blk", None, None), P("event", "blk", None, None), P())
    return jax.shard_map(
        per_device, mesh=mesh, in_specs=in_specs, out_specs=out_specs, check_vma=False
    )
```

```python
import jax
import jax.numpy as jnp
from jax import lax
from jax.experimental import pallas as pl
from jax.experimental.pallas import tpu as pltpu
from jax.sharding import PartitionSpec as P

CHANNELS = 64
EDGE = 8
VOXELS = 512
FACE = EDGE * EDGE
TAPS = 27
GRID_Y = 8
GRID_Z = 8
ACTIVE = 24
PAIR = 2 * CHANNELS
HALF = TAPS // 2 + 1


def turned(face):
    face = face.astype(jnp.float32)
    return jnp.concatenate([face[:, :FACE], face[:, FACE:]], axis=0).T


def corner(q):
    return lax.div(q, GRID_Z) * EDGE, pl.multiple_of(lax.rem(q, GRID_Z) * EDGE, EDGE)


def kernel(
    slots, cells, x_ref, g_ref, occ_ref, w_ref,
    out_ref, back_ref, gw_ref,
    plane, cols, rows_ref, sums, taps_ref, table, low, high,
    face_lo, face_hi, in_lo, in_hi, flat, parts, got, terms, whole,
    send_b, recv_b, send_e, recv_e, send_g, recv_g, send_f, recv_f,
):
    blk, event = lax.axis_index("blk"), lax.axis_index("event")
    blks, events = lax.axis_size("blk"), lax.axis_size("event")

    def near(k):
        return lax.rem(blk + k, blks)

    def far(k):
        return lax.rem(event + k, events)

    def send(src, dst, out_sem, in_sem, target):
        copy = pltpu.make_async_remote_copy(
            src_ref=src,
            dst_ref=dst,
            send_sem=out_sem,
            recv_sem=in_sem,
            device_id=target,
            device_id_type=pl.DeviceIdType.MESH,
        )
        copy.start()
        return copy

    barrier = pltpu.get_barrier_semaphore()
    for k in range(1, blks):
        pl.semaphore_signal(
            barrier, inc=1, device_id=(event, near(k)), device_id_type=pl.DeviceIdType.MESH
        )
    for k in range(1, events):
        pl.semaphore_signal(
            barrier, inc=1, device_id=(far(k), blk), device_id_type=pl.DeviceIdType.MESH
        )

    def masked(b, span):
        mask = occ_ref[pl.ds(b, 1), :].astype(jnp.float32)[:, span]
        return (
            x_ref[b, :, span].astype(jnp.float32) * mask,
            g_ref[b, :, span].astype(jnp.float32) * mask,
        )

    def make_faces(b, _):
        x, g = masked(b, slice(0, PAIR))
        face_lo[b] = jnp.concatenate([x[:, :FACE], g[:, :FACE]], axis=1).astype(jnp.bfloat16)
        x, g = masked(b, slice(VOXELS - PAIR, VOXELS))
        face_hi[b] = jnp.concatenate([x[:, FACE:], g[:, FACE:]], axis=1).astype(jnp.bfloat16)
        return 0

    lax.fori_loop(0, ACTIVE, make_faces, 0)
    pl.semaphore_wait(barrier, blks + events - 2)
    halo = [
        send(face_hi, in_lo, send_f.at[0], recv_f.at[0], (event, near(1))),
        send(face_lo, in_hi, send_f.at[1], recv_f.at[1], (event, near(blks - 1))),
    ]

    def clear(i, _):
        plane[i, 0] = jnp.zeros(plane.shape[2:], plane.dtype)
        plane[i, GRID_Y * EDGE + 1] = jnp.zeros(plane.shape[2:], plane.dtype)
        edge = jnp.zeros((GRID_Y * EDGE + 2, EDGE, PAIR), plane.dtype)
        plane[i, :, :EDGE, :] = edge
        plane[i, :, (GRID_Z + 1) * EDGE :, :] = edge
        return 0

    lax.fori_loop(0, EDGE + 2, clear, 0)
    sums[...] = jnp.zeros(sums.shape, sums.dtype)
    table[ACTIVE] = jnp.zeros(table.shape[1:], table.dtype)
    low[ACTIVE] = jnp.zeros(low.shape[1:], low.dtype)
    high[ACTIVE] = jnp.zeros(high.shape[1:], high.dtype)
    none = jnp.zeros((CHANNELS, CHANNELS), jnp.float32)
    for t in range(TAPS):
        a, at = t // 9, t % 9 * PAIR
        ahead = w_ref[t].astype(jnp.float32)
        behind = w_ref[TAPS - 1 - t].astype(jnp.float32).T
        taps_ref[a, at : at + CHANNELS] = jnp.concatenate([ahead, none], axis=1).astype(jnp.bfloat16)
        taps_ref[a, at + CHANNELS : at + PAIR] = jnp.concatenate([none, behind], axis=1).astype(
            jnp.bfloat16
        )

    def prepare(b, _):
        both = jnp.concatenate(masked(b, slice(0, VOXELS)), axis=0)
        rows_ref[b] = both.astype(jnp.bfloat16)
        table[b] = both.T
        return 0

    lax.fori_loop(0, ACTIVE, prepare, 0)

    def fill(q, _):
        y, z = corner(q)
        plane[1 : EDGE + 1, pl.ds(y + 1, EDGE), pl.ds(z + EDGE, EDGE), :] = table[
            slots[1, q]
        ].reshape(EDGE, EDGE, EDGE, PAIR)
        return 0

    lax.fori_loop(0, GRID_Y * GRID_Z, fill, 0)
    for copy in halo:
        copy.wait()

    def turn(b, _):
        low[b] = turned(in_lo[b])
        high[b] = turned(in_hi[b])
        return 0

    lax.fori_loop(0, ACTIVE, turn, 0)

    def fill_faces(q, _):
        y, z = corner(q)
        for layer, faces, at in ((0, low, 0), (2, high, EDGE + 1)):
            plane[at, pl.ds(y + 1, EDGE), pl.ds(z + EDGE, EDGE), :] = faces[
                slots[layer, q]
            ].reshape(EDGE, EDGE, PAIR)
        return 0

    lax.fori_loop(0, GRID_Y * GRID_Z, fill_faces, 0)

    def spread(b):
        y, z = cells[0, b] * EDGE, cells[1, b] * EDGE
        for c in range(3):
            for e in range(3):
                part = plane[:, pl.ds(y + c, EDGE), pl.ds(z + EDGE - 1 + e, EDGE), :]
                at = (3 * c + e) * PAIR
                cols[:, at : at + PAIR] = part.reshape((EDGE + 2) * FACE, PAIR).astype(jnp.bfloat16)

    def gradient(b, _):
        spread(b)
        rows = rows_ref[b]
        sums[:, : 5 * PAIR] += jnp.dot(
            rows, cols[FACE : FACE + VOXELS, 4 * PAIR :], preferred_element_type=jnp.float32
        )
        sums[:, 5 * PAIR :] += jnp.dot(
            rows, cols[2 * FACE :, :], preferred_element_type=jnp.float32
        )
        return 0

    def convolve(b, _):
        spread(b)
        total = jnp.dot(cols[:VOXELS, :], taps_ref[0], preferred_element_type=jnp.float32)
        for a in (1, 2):
            total += jnp.dot(
                cols[a * FACE : a * FACE + VOXELS, :],
                taps_ref[a],
                preferred_element_type=jnp.float32,
            )
        mask = occ_ref[pl.ds(b, 1), :].astype(jnp.float32)
        result = (total.T * mask).astype(jnp.bfloat16)
        out_ref[b] = result[:CHANNELS]
        back_ref[b] = result[CHANNELS:]
        return 0

    lax.fori_loop(0, ACTIVE, gradient, 0)
    for n in range(HALF):
        at = n * PAIR
        flat[n * CHANNELS : (n + 1) * CHANNELS] = jnp.concatenate(
            [
                sums[CHANNELS:, at : at + PAIR].T[:CHANNELS],
                sums[:CHANNELS, at + CHANNELS : at + PAIR],
            ],
            axis=1,
        )
    size = parts.shape[1]
    for k in range(blks):
        parts[k] = flat[k * size : (k + 1) * size]

    third = ACTIVE // 3
    copies = [
        send(parts.at[near(k)], got.at[k - 1], send_b.at[k], recv_b.at[k], (event, near(k)))
        for k in range(1, blks)
    ]
    lax.fori_loop(0, third, convolve, 0)
    total = parts[blk]
    for k, copy in enumerate(copies):
        copy.wait()
        total += got[k]
    terms[event] = total
    copies = [
        send(terms.at[event], terms.at[event], send_e.at[k], recv_e.at[k], (far(k), blk))
        for k in range(1, events)
    ]
    lax.fori_loop(third, 2 * third, convolve, 0)
    for copy in copies:
        copy.wait()
    total = terms[0]
    for k in range(1, events):
        total += terms[k]
    whole[blk] = total
    copies = [
        send(whole.at[blk], whole.at[blk], send_g.at[k], recv_g.at[k], (event, near(k)))
        for k in range(1, blks)
    ]
    lax.fori_loop(2 * third, ACTIVE, convolve, 0)
    for copy in copies:
        copy.wait()
    gw_ref[...] = whole[...]


def per_device(features, occupancy, block_cells, weight, cotangent):
    device = lax.axis_index("blk")
    blks, events = lax.axis_size("blk"), lax.axis_size("event")
    x, g, occ = features[0], cotangent[0], occupancy[0]
    planes = block_cells[0].reshape(blks, ACTIVE)
    hits = planes[:, None, :] == jnp.arange(GRID_Y * GRID_Z, dtype=jnp.int32)[None, :, None]
    listing = jnp.arange(ACTIVE, dtype=jnp.int32) - ACTIVE
    slots = ACTIVE + jnp.sum(jnp.where(hits, listing, 0), axis=-1)
    slots = jnp.pad(slots, ((1, 1), (0, 0)), constant_values=ACTIVE)
    slots = lax.dynamic_slice_in_dim(slots, device, 3).astype(jnp.int32)
    cells = lax.dynamic_slice_in_dim(block_cells[0], device * ACTIVE, ACTIVE)
    cells = jnp.stack([lax.div(cells, GRID_Z), lax.rem(cells, GRID_Z)])
    part = (HALF * CHANNELS // blks, PAIR)
    vmem = pl.BlockSpec(memory_space=pltpu.VMEM)
    smem = pl.BlockSpec(memory_space=pltpu.SMEM)
    wide, half = jnp.float32, jnp.bfloat16
    face = (ACTIVE, CHANNELS, PAIR)
    output, back, terms = pl.pallas_call(
        kernel,
        out_shape=[
            jax.ShapeDtypeStruct(x.shape, x.dtype),
            jax.ShapeDtypeStruct(x.shape, x.dtype),
            jax.ShapeDtypeStruct((blks,) + part, wide),
        ],
        in_specs=[smem, smem, vmem, vmem, vmem, vmem],
        out_specs=[vmem] * 3,
        scratch_shapes=[
            pltpu.VMEM((EDGE + 2, GRID_Y * EDGE + 2, (GRID_Z + 2) * EDGE, PAIR), wide),
            pltpu.VMEM(((EDGE + 2) * FACE, 9 * PAIR), half),
            pltpu.VMEM((ACTIVE, PAIR, VOXELS), half),
            pltpu.VMEM((PAIR, HALF * PAIR), wide),
            pltpu.VMEM((3, 9 * PAIR, PAIR), half),
            pltpu.VMEM((ACTIVE + 1, VOXELS, PAIR), wide),
            pltpu.VMEM((ACTIVE + 1, FACE, PAIR), wide),
            pltpu.VMEM((ACTIVE + 1, FACE, PAIR), wide),
            pltpu.VMEM(face, half),
            pltpu.VMEM(face, half),
            pltpu.VMEM(face, half),
            pltpu.VMEM(face, half),
            pltpu.VMEM((HALF * CHANNELS, PAIR), wide),
            pltpu.VMEM((blks,) + part, wide),
            pltpu.VMEM((blks - 1,) + part, wide),
            pltpu.VMEM((events,) + part, wide),
            pltpu.VMEM((blks,) + part, wide),
        ]
        + [
            pltpu.SemaphoreType.DMA((n,))
            for n in (blks, blks, events, events, blks, blks, 2, 2)
        ],
        cost_estimate=pl.CostEstimate(
            flops=2 * ACTIVE * VOXELS * TAPS * CHANNELS * CHANNELS * 3,
            bytes_accessed=8 * x.size,
            transcendentals=0,
        ),
        compiler_params=pltpu.CompilerParams(
            vmem_limit_bytes=58 * 1024 * 1024, collective_id=0, has_side_effects=True
        ),
    )(slots, cells, x, g, occ, weight)
    terms = terms.reshape(HALF, CHANNELS, PAIR)
    grad_weight = jnp.concatenate([terms[:0:-1, :, CHANNELS:], terms[:, :, :CHANNELS]], axis=0)
    return (output[None], back[None], grad_weight)


def solution(mesh):
    in_specs = (
        P("event", "blk", None, None),
        P("event", "blk", None),
        P("event", None),
        P(),
        P("event", "blk", None, None),
    )
    out_specs = (P("event", "blk", None, None), P("event", "blk", None, None), P())
    return jax.shard_map(
        per_device, mesh=mesh, in_specs=in_specs, out_specs=out_specs, check_vma=False
    )
```

```python
import jax
import jax.numpy as jnp
from jax import lax
from jax.experimental import pallas as pl
from jax.experimental.pallas import tpu as pltpu
from jax.sharding import PartitionSpec as P

CHANNELS = 64
EDGE = 8
VOXELS = 512
FACE = EDGE * EDGE
TAPS = 27
GRID_Y = 8
GRID_Z = 8
ACTIVE = 24
PAIR = 2 * CHANNELS
HALF = TAPS // 2 + 1


def turned(face):
    face = face.astype(jnp.float32)
    return jnp.concatenate([face[:, :FACE], face[:, FACE:]], axis=0).T


def corner(q):
    return lax.div(q, GRID_Z) * EDGE, pl.multiple_of(lax.rem(q, GRID_Z) * EDGE, EDGE)


def kernel(
    slots, cells, x_ref, g_ref, occ_ref, w_ref,
    out_ref, back_ref, gw_ref,
    plane, cols, rows_ref, sums, taps_ref, table, low, high,
    face_lo, face_hi, in_lo, in_hi, flat, parts, got, terms, whole,
    send_b, recv_b, send_e, recv_e, send_g, recv_g, send_f, recv_f,
):
    blk, event = lax.axis_index("blk"), lax.axis_index("event")
    blks, events = lax.axis_size("blk"), lax.axis_size("event")

    def near(k):
        return lax.rem(blk + k, blks)

    def far(k):
        return lax.rem(event + k, events)

    def send(src, dst, out_sem, in_sem, target):
        copy = pltpu.make_async_remote_copy(
            src_ref=src,
            dst_ref=dst,
            send_sem=out_sem,
            recv_sem=in_sem,
            device_id=target,
            device_id_type=pl.DeviceIdType.MESH,
        )
        copy.start()
        return copy

    barrier = pltpu.get_barrier_semaphore()
    for k in range(1, blks):
        pl.semaphore_signal(
            barrier, inc=1, device_id=(event, near(k)), device_id_type=pl.DeviceIdType.MESH
        )
    for k in range(1, events):
        pl.semaphore_signal(
            barrier, inc=1, device_id=(far(k), blk), device_id_type=pl.DeviceIdType.MESH
        )

    def masked(b, span):
        mask = occ_ref[pl.ds(b, 1), :].astype(jnp.float32)[:, span]
        return (
            x_ref[b, :, span].astype(jnp.float32) * mask,
            g_ref[b, :, span].astype(jnp.float32) * mask,
        )

    def make_faces(b, _):
        x, g = masked(b, slice(0, PAIR))
        face_lo[b] = jnp.concatenate([x[:, :FACE], g[:, :FACE]], axis=1).astype(jnp.bfloat16)
        x, g = masked(b, slice(VOXELS - PAIR, VOXELS))
        face_hi[b] = jnp.concatenate([x[:, FACE:], g[:, FACE:]], axis=1).astype(jnp.bfloat16)
        return 0

    lax.fori_loop(0, ACTIVE, make_faces, 0)
    pl.semaphore_wait(barrier, blks + events - 2)
    halo = [
        send(face_hi, in_lo, send_f.at[0], recv_f.at[0], (event, near(1))),
        send(face_lo, in_hi, send_f.at[1], recv_f.at[1], (event, near(blks - 1))),
    ]

    def clear(i, _):
        plane[i, 0] = jnp.zeros(plane.shape[2:], plane.dtype)
        plane[i, GRID_Y * EDGE + 1] = jnp.zeros(plane.shape[2:], plane.dtype)
        edge = jnp.zeros((GRID_Y * EDGE + 2, EDGE, PAIR), plane.dtype)
        plane[i, :, :EDGE, :] = edge
        plane[i, :, (GRID_Z + 1) * EDGE :, :] = edge
        return 0

    lax.fori_loop(0, EDGE + 2, clear, 0)
    sums[...] = jnp.zeros(sums.shape, sums.dtype)
    table[ACTIVE] = jnp.zeros(table.shape[1:], table.dtype)
    low[ACTIVE] = jnp.zeros(low.shape[1:], low.dtype)
    high[ACTIVE] = jnp.zeros(high.shape[1:], high.dtype)
    none = jnp.zeros((CHANNELS, CHANNELS), jnp.float32)
    for t in range(TAPS):
        a, at = t // 9, t % 9 * PAIR
        ahead = w_ref[t].astype(jnp.float32)
        behind = w_ref[TAPS - 1 - t].astype(jnp.float32).T
        to = slice(a * PAIR, (a + 1) * PAIR)
        taps_ref[at : at + CHANNELS, to] = jnp.concatenate([ahead, none], axis=1).astype(jnp.bfloat16)
        taps_ref[at + CHANNELS : at + PAIR, to] = jnp.concatenate([none, behind], axis=1).astype(
            jnp.bfloat16
        )

    def prepare(b, _):
        both = jnp.concatenate(masked(b, slice(0, VOXELS)), axis=0)
        rows_ref[b] = both.astype(jnp.bfloat16)
        table[b] = both.T
        return 0

    lax.fori_loop(0, ACTIVE, prepare, 0)

    def fill(q, _):
        y, z = corner(q)
        plane[1 : EDGE + 1, pl.ds(y + 1, EDGE), pl.ds(z + EDGE, EDGE), :] = table[
            slots[1, q]
        ].reshape(EDGE, EDGE, EDGE, PAIR)
        return 0

    lax.fori_loop(0, GRID_Y * GRID_Z, fill, 0)
    for copy in halo:
        copy.wait()

    def turn(b, _):
        low[b] = turned(in_lo[b])
        high[b] = turned(in_hi[b])
        return 0

    lax.fori_loop(0, ACTIVE, turn, 0)

    def fill_faces(q, _):
        y, z = corner(q)
        for layer, faces, at in ((0, low, 0), (2, high, EDGE + 1)):
            plane[at, pl.ds(y + 1, EDGE), pl.ds(z + EDGE, EDGE), :] = faces[
                slots[layer, q]
            ].reshape(EDGE, EDGE, PAIR)
        return 0

    lax.fori_loop(0, GRID_Y * GRID_Z, fill_faces, 0)

    def spread(b):
        y, z = cells[0, b] * EDGE, cells[1, b] * EDGE
        for c in range(3):
            for e in range(3):
                part = plane[:, pl.ds(y + c, EDGE), pl.ds(z + EDGE - 1 + e, EDGE), :]
                at = (3 * c + e) * PAIR
                cols[:, at : at + PAIR] = part.reshape((EDGE + 2) * FACE, PAIR).astype(jnp.bfloat16)

    def gradient(b, _):
        spread(b)
        rows = rows_ref[b]
        sums[:, : 5 * PAIR] += jnp.dot(
            rows, cols[FACE : FACE + VOXELS, 4 * PAIR :], preferred_element_type=jnp.float32
        )
        sums[:, 5 * PAIR :] += jnp.dot(
            rows, cols[2 * FACE :, :], preferred_element_type=jnp.float32
        )
        return 0

    def convolve(b, _):
        spread(b)
        double = jnp.dot(
            cols[: VOXELS + FACE, :], taps_ref[:, : 2 * PAIR], preferred_element_type=jnp.float32
        )
        total = double[:VOXELS, :PAIR] + double[FACE:, PAIR:]
        total += jnp.dot(
            cols[2 * FACE :, :], taps_ref[:, 2 * PAIR :], preferred_element_type=jnp.float32
        )
        mask = occ_ref[pl.ds(b, 1), :].astype(jnp.float32)
        result = (total.T * mask).astype(jnp.bfloat16)
        out_ref[b] = result[:CHANNELS]
        back_ref[b] = result[CHANNELS:]
        return 0

    lax.fori_loop(0, ACTIVE, gradient, 0)
    for n in range(HALF):
        at = n * PAIR
        flat[n * CHANNELS : (n + 1) * CHANNELS] = jnp.concatenate(
            [
                sums[CHANNELS:, at : at + PAIR].T[:CHANNELS],
                sums[:CHANNELS, at + CHANNELS : at + PAIR],
            ],
            axis=1,
        )
    size = parts.shape[1]
    for k in range(blks):
        parts[k] = flat[k * size : (k + 1) * size]

    third = ACTIVE // 3
    copies = [
        send(parts.at[near(k)], got.at[k - 1], send_b.at[k], recv_b.at[k], (event, near(k)))
        for k in range(1, blks)
    ]
    lax.fori_loop(0, third, convolve, 0)
    total = parts[blk]
    for k, copy in enumerate(copies):
        copy.wait()
        total += got[k]
    terms[event] = total
    copies = [
        send(terms.at[event], terms.at[event], send_e.at[k], recv_e.at[k], (far(k), blk))
        for k in range(1, events)
    ]
    lax.fori_loop(third, 2 * third, convolve, 0)
    for copy in copies:
        copy.wait()
    total = terms[0]
    for k in range(1, events):
        total += terms[k]
    whole[blk] = total
    copies = [
        send(whole.at[blk], whole.at[blk], send_g.at[k], recv_g.at[k], (event, near(k)))
        for k in range(1, blks)
    ]
    lax.fori_loop(2 * third, ACTIVE, convolve, 0)
    for copy in copies:
        copy.wait()
    gw_ref[...] = whole[...]


def per_device(features, occupancy, block_cells, weight, cotangent):
    device = lax.axis_index("blk")
    blks, events = lax.axis_size("blk"), lax.axis_size("event")
    x, g, occ = features[0], cotangent[0], occupancy[0]
    planes = block_cells[0].reshape(blks, ACTIVE)
    hits = planes[:, None, :] == jnp.arange(GRID_Y * GRID_Z, dtype=jnp.int32)[None, :, None]
    listing = jnp.arange(ACTIVE, dtype=jnp.int32) - ACTIVE
    slots = ACTIVE + jnp.sum(jnp.where(hits, listing, 0), axis=-1)
    slots = jnp.pad(slots, ((1, 1), (0, 0)), constant_values=ACTIVE)
    slots = lax.dynamic_slice_in_dim(slots, device, 3).astype(jnp.int32)
    cells = lax.dynamic_slice_in_dim(block_cells[0], device * ACTIVE, ACTIVE)
    cells = jnp.stack([lax.div(cells, GRID_Z), lax.rem(cells, GRID_Z)])
    part = (HALF * CHANNELS // blks, PAIR)
    vmem = pl.BlockSpec(memory_space=pltpu.VMEM)
    smem = pl.BlockSpec(memory_space=pltpu.SMEM)
    wide, half = jnp.float32, jnp.bfloat16
    face = (ACTIVE, CHANNELS, PAIR)
    output, back, terms = pl.pallas_call(
        kernel,
        out_shape=[
            jax.ShapeDtypeStruct(x.shape, x.dtype),
            jax.ShapeDtypeStruct(x.shape, x.dtype),
            jax.ShapeDtypeStruct((blks,) + part, wide),
        ],
        in_specs=[smem, smem, vmem, vmem, vmem, vmem],
        out_specs=[vmem] * 3,
        scratch_shapes=[
            pltpu.VMEM((EDGE + 2, GRID_Y * EDGE + 2, (GRID_Z + 2) * EDGE, PAIR), wide),
            pltpu.VMEM(((EDGE + 2) * FACE, 9 * PAIR), half),
            pltpu.VMEM((ACTIVE, PAIR, VOXELS), half),
            pltpu.VMEM((PAIR, HALF * PAIR), wide),
            pltpu.VMEM((9 * PAIR, 3 * PAIR), half),
            pltpu.VMEM((ACTIVE + 1, VOXELS, PAIR), wide),
            pltpu.VMEM((ACTIVE + 1, FACE, PAIR), wide),
            pltpu.VMEM((ACTIVE + 1, FACE, PAIR), wide),
            pltpu.VMEM(face, half),
            pltpu.VMEM(face, half),
            pltpu.VMEM(face, half),
            pltpu.VMEM(face, half),
            pltpu.VMEM((HALF * CHANNELS, PAIR), wide),
            pltpu.VMEM((blks,) + part, wide),
            pltpu.VMEM((blks - 1,) + part, wide),
            pltpu.VMEM((events,) + part, wide),
            pltpu.VMEM((blks,) + part, wide),
        ]
        + [
            pltpu.SemaphoreType.DMA((n,))
            for n in (blks, blks, events, events, blks, blks, 2, 2)
        ],
        cost_estimate=pl.CostEstimate(
            flops=2 * ACTIVE * VOXELS * TAPS * CHANNELS * CHANNELS * 3,
            bytes_accessed=8 * x.size,
            transcendentals=0,
        ),
        compiler_params=pltpu.CompilerParams(
            vmem_limit_bytes=58 * 1024 * 1024, collective_id=0, has_side_effects=True
        ),
    )(slots, cells, x, g, occ, weight)
    terms = terms.reshape(HALF, CHANNELS, PAIR)
    grad_weight = jnp.concatenate([terms[:0:-1, :, CHANNELS:], terms[:, :, :CHANNELS]], axis=0)
    return (output[None], back[None], grad_weight)


def solution(mesh):
    in_specs = (
        P("event", "blk", None, None),
        P("event", "blk", None),
        P("event", None),
        P(),
        P("event", "blk", None, None),
    )
    out_specs = (P("event", "blk", None, None), P("event", "blk", None, None), P())
    return jax.shard_map(
        per_device, mesh=mesh, in_specs=in_specs, out_specs=out_specs, check_vma=False
    )
```

```python
import jax
import jax.numpy as jnp
from jax import lax
from jax.experimental import pallas as pl
from jax.experimental.pallas import tpu as pltpu
from jax.sharding import PartitionSpec as P

CHANNELS = 64
EDGE = 8
VOXELS = 512
FACE = EDGE * EDGE
TAPS = 27
GRID_Y = 8
GRID_Z = 8
ACTIVE = 24
PAIR = 2 * CHANNELS
HALF = TAPS // 2 + 1


def turned(face):
    face = face.astype(jnp.float32)
    return jnp.concatenate([face[:, :FACE], face[:, FACE:]], axis=0).T


def corner(q):
    return lax.div(q, GRID_Z) * EDGE, pl.multiple_of(lax.rem(q, GRID_Z) * EDGE, EDGE)


def kernel(
    slots, cells, x_ref, g_ref, occ_ref, w_ref,
    out_ref, back_ref, gw_ref,
    plane, cols, rows_ref, sums, taps_ref, table, low, high,
    face_lo, face_hi, in_lo, in_hi, flat, parts, got, terms, whole,
    send_b, recv_b, send_e, recv_e, send_g, recv_g, send_f, recv_f,
):
    blk, event = lax.axis_index("blk"), lax.axis_index("event")
    blks, events = lax.axis_size("blk"), lax.axis_size("event")

    def near(k):
        return lax.rem(blk + k, blks)

    def far(k):
        return lax.rem(event + k, events)

    def send(src, dst, out_sem, in_sem, target):
        copy = pltpu.make_async_remote_copy(
            src_ref=src,
            dst_ref=dst,
            send_sem=out_sem,
            recv_sem=in_sem,
            device_id=target,
            device_id_type=pl.DeviceIdType.MESH,
        )
        copy.start()
        return copy

    barrier = pltpu.get_barrier_semaphore()
    for k in range(1, blks):
        pl.semaphore_signal(
            barrier, inc=1, device_id=(event, near(k)), device_id_type=pl.DeviceIdType.MESH
        )
    for k in range(1, events):
        pl.semaphore_signal(
            barrier, inc=1, device_id=(far(k), blk), device_id_type=pl.DeviceIdType.MESH
        )

    def masked(b, span):
        mask = occ_ref[pl.ds(b, 1), :].astype(jnp.float32)[:, span]
        return (
            x_ref[b, :, span].astype(jnp.float32) * mask,
            g_ref[b, :, span].astype(jnp.float32) * mask,
        )

    def make_faces(b, _):
        x, g = masked(b, slice(0, PAIR))
        face_lo[b] = jnp.concatenate([x[:, :FACE], g[:, :FACE]], axis=1).astype(jnp.bfloat16)
        x, g = masked(b, slice(VOXELS - PAIR, VOXELS))
        face_hi[b] = jnp.concatenate([x[:, FACE:], g[:, FACE:]], axis=1).astype(jnp.bfloat16)
        return 0

    lax.fori_loop(0, ACTIVE, make_faces, 0)
    pl.semaphore_wait(barrier, blks + events - 2)
    halo = [
        send(face_hi, in_lo, send_f.at[0], recv_f.at[0], (event, near(1))),
        send(face_lo, in_hi, send_f.at[1], recv_f.at[1], (event, near(blks - 1))),
    ]

    def clear(i, _):
        plane[i, 0] = jnp.zeros(plane.shape[2:], plane.dtype)
        plane[i, GRID_Y * EDGE + 1] = jnp.zeros(plane.shape[2:], plane.dtype)
        edge = jnp.zeros((GRID_Y * EDGE + 2, EDGE, PAIR), plane.dtype)
        plane[i, :, :EDGE, :] = edge
        plane[i, :, (GRID_Z + 1) * EDGE :, :] = edge
        return 0

    lax.fori_loop(0, EDGE + 2, clear, 0)
    sums[...] = jnp.zeros(sums.shape, sums.dtype)
    table[ACTIVE] = jnp.zeros(table.shape[1:], table.dtype)
    low[ACTIVE] = jnp.zeros(low.shape[1:], low.dtype)
    high[ACTIVE] = jnp.zeros(high.shape[1:], high.dtype)
    none = jnp.zeros((CHANNELS, CHANNELS), jnp.float32)
    for t in range(TAPS):
        a, at = t // 9, t % 9 * PAIR
        ahead = w_ref[t].astype(jnp.float32)
        behind = w_ref[TAPS - 1 - t].astype(jnp.float32).T
        to = slice(a * PAIR, (a + 1) * PAIR)
        taps_ref[at : at + CHANNELS, to] = jnp.concatenate([ahead, none], axis=1).astype(jnp.bfloat16)
        taps_ref[at + CHANNELS : at + PAIR, to] = jnp.concatenate([none, behind], axis=1).astype(
            jnp.bfloat16
        )

    def prepare(b, _):
        both = jnp.concatenate(masked(b, slice(0, VOXELS)), axis=0)
        rows_ref[b] = both.astype(jnp.bfloat16)
        table[b] = both.T
        return 0

    lax.fori_loop(0, ACTIVE, prepare, 0)

    def fill(q, _):
        y, z = corner(q)
        plane[1 : EDGE + 1, pl.ds(y + 1, EDGE), pl.ds(z + EDGE, EDGE), :] = table[
            slots[1, q]
        ].reshape(EDGE, EDGE, EDGE, PAIR)
        return 0

    lax.fori_loop(0, GRID_Y * GRID_Z, fill, 0)
    for copy in halo:
        copy.wait()

    def turn(b, _):
        low[b] = turned(in_lo[b])
        high[b] = turned(in_hi[b])
        return 0

    lax.fori_loop(0, ACTIVE, turn, 0)

    def fill_faces(q, _):
        y, z = corner(q)
        for layer, faces, at in ((0, low, 0), (2, high, EDGE + 1)):
            plane[at, pl.ds(y + 1, EDGE), pl.ds(z + EDGE, EDGE), :] = faces[
                slots[layer, q]
            ].reshape(EDGE, EDGE, PAIR)
        return 0

    lax.fori_loop(0, GRID_Y * GRID_Z, fill_faces, 0)

    def spread(b, cols):
        y, z = cells[0, b] * EDGE, cells[1, b] * EDGE
        for c in range(3):
            for e in range(3):
                part = plane[:, pl.ds(y + c, EDGE), pl.ds(z + EDGE - 1 + e, EDGE), :]
                at = (3 * c + e) * PAIR
                cols[:, at : at + PAIR] = part.reshape((EDGE + 2) * FACE, PAIR).astype(jnp.bfloat16)

    def gradient(b, cols):
        rows = rows_ref[b]
        sums[:, : 5 * PAIR] += jnp.dot(
            rows, cols[FACE : FACE + VOXELS, 4 * PAIR :], preferred_element_type=jnp.float32
        )
        sums[:, 5 * PAIR :] += jnp.dot(
            rows, cols[2 * FACE :, :], preferred_element_type=jnp.float32
        )

    def convolve(b, cols):
        double = jnp.dot(
            cols[: VOXELS + FACE, :], taps_ref[:, : 2 * PAIR], preferred_element_type=jnp.float32
        )
        total = double[:VOXELS, :PAIR] + double[FACE:, PAIR:]
        total += jnp.dot(
            cols[2 * FACE :, :], taps_ref[:, 2 * PAIR :], preferred_element_type=jnp.float32
        )
        mask = occ_ref[pl.ds(b, 1), :].astype(jnp.float32)
        result = (total.T * mask).astype(jnp.bfloat16)
        out_ref[b] = result[:CHANNELS]
        back_ref[b] = result[CHANNELS:]

    def paired(work, start, stop):
        def step(i, _):
            spread(2 * i, cols.at[0])
            spread(2 * i + 1, cols.at[1])
            work(2 * i, cols.at[0])
            work(2 * i + 1, cols.at[1])
            return 0

        lax.fori_loop(start // 2, stop // 2, step, 0)

    paired(gradient, 0, ACTIVE)
    for n in range(HALF):
        at = n * PAIR
        flat[n * CHANNELS : (n + 1) * CHANNELS] = jnp.concatenate(
            [
                sums[CHANNELS:, at : at + PAIR].T[:CHANNELS],
                sums[:CHANNELS, at + CHANNELS : at + PAIR],
            ],
            axis=1,
        )
    size = parts.shape[1]
    for k in range(blks):
        parts[k] = flat[k * size : (k + 1) * size]

    third = ACTIVE // 3
    copies = [
        send(parts.at[near(k)], got.at[k - 1], send_b.at[k], recv_b.at[k], (event, near(k)))
        for k in range(1, blks)
    ]
    paired(convolve, 0, third)
    total = parts[blk]
    for k, copy in enumerate(copies):
        copy.wait()
        total += got[k]
    terms[event] = total
    copies = [
        send(terms.at[event], terms.at[event], send_e.at[k], recv_e.at[k], (far(k), blk))
        for k in range(1, events)
    ]
    paired(convolve, third, 2 * third)
    for copy in copies:
        copy.wait()
    total = terms[0]
    for k in range(1, events):
        total += terms[k]
    whole[blk] = total
    copies = [
        send(whole.at[blk], whole.at[blk], send_g.at[k], recv_g.at[k], (event, near(k)))
        for k in range(1, blks)
    ]
    paired(convolve, 2 * third, ACTIVE)
    for copy in copies:
        copy.wait()
    gw_ref[...] = whole[...]


def per_device(features, occupancy, block_cells, weight, cotangent):
    device = lax.axis_index("blk")
    blks, events = lax.axis_size("blk"), lax.axis_size("event")
    x, g, occ = features[0], cotangent[0], occupancy[0]
    planes = block_cells[0].reshape(blks, ACTIVE)
    hits = planes[:, None, :] == jnp.arange(GRID_Y * GRID_Z, dtype=jnp.int32)[None, :, None]
    listing = jnp.arange(ACTIVE, dtype=jnp.int32) - ACTIVE
    slots = ACTIVE + jnp.sum(jnp.where(hits, listing, 0), axis=-1)
    slots = jnp.pad(slots, ((1, 1), (0, 0)), constant_values=ACTIVE)
    slots = lax.dynamic_slice_in_dim(slots, device, 3).astype(jnp.int32)
    cells = lax.dynamic_slice_in_dim(block_cells[0], device * ACTIVE, ACTIVE)
    cells = jnp.stack([lax.div(cells, GRID_Z), lax.rem(cells, GRID_Z)])
    part = (HALF * CHANNELS // blks, PAIR)
    vmem = pl.BlockSpec(memory_space=pltpu.VMEM)
    smem = pl.BlockSpec(memory_space=pltpu.SMEM)
    wide, half = jnp.float32, jnp.bfloat16
    face = (ACTIVE, CHANNELS, PAIR)
    output, back, terms = pl.pallas_call(
        kernel,
        out_shape=[
            jax.ShapeDtypeStruct(x.shape, x.dtype),
            jax.ShapeDtypeStruct(x.shape, x.dtype),
            jax.ShapeDtypeStruct((blks,) + part, wide),
        ],
        in_specs=[smem, smem, vmem, vmem, vmem, vmem],
        out_specs=[vmem] * 3,
        scratch_shapes=[
            pltpu.VMEM((EDGE + 2, GRID_Y * EDGE + 2, (GRID_Z + 2) * EDGE, PAIR), wide),
            pltpu.VMEM((2, (EDGE + 2) * FACE, 9 * PAIR), half),
            pltpu.VMEM((ACTIVE, PAIR, VOXELS), half),
            pltpu.VMEM((PAIR, HALF * PAIR), wide),
            pltpu.VMEM((9 * PAIR, 3 * PAIR), half),
            pltpu.VMEM((ACTIVE + 1, VOXELS, PAIR), wide),
            pltpu.VMEM((ACTIVE + 1, FACE, PAIR), wide),
            pltpu.VMEM((ACTIVE + 1, FACE, PAIR), wide),
            pltpu.VMEM(face, half),
            pltpu.VMEM(face, half),
            pltpu.VMEM(face, half),
            pltpu.VMEM(face, half),
            pltpu.VMEM((HALF * CHANNELS, PAIR), wide),
            pltpu.VMEM((blks,) + part, wide),
            pltpu.VMEM((blks - 1,) + part, wide),
            pltpu.VMEM((events,) + part, wide),
            pltpu.VMEM((blks,) + part, wide),
        ]
        + [
            pltpu.SemaphoreType.DMA((n,))
            for n in (blks, blks, events, events, blks, blks, 2, 2)
        ],
        cost_estimate=pl.CostEstimate(
            flops=2 * ACTIVE * VOXELS * TAPS * CHANNELS * CHANNELS * 3,
            bytes_accessed=8 * x.size,
            transcendentals=0,
        ),
        compiler_params=pltpu.CompilerParams(
            vmem_limit_bytes=58 * 1024 * 1024, collective_id=0, has_side_effects=True
        ),
    )(slots, cells, x, g, occ, weight)
    terms = terms.reshape(HALF, CHANNELS, PAIR)
    grad_weight = jnp.concatenate([terms[:0:-1, :, CHANNELS:], terms[:, :, :CHANNELS]], axis=0)
    return (output[None], back[None], grad_weight)


def solution(mesh):
    in_specs = (
        P("event", "blk", None, None),
        P("event", "blk", None),
        P("event", None),
        P(),
        P("event", "blk", None, None),
    )
    out_specs = (P("event", "blk", None, None), P("event", "blk", None, None), P())
    return jax.shard_map(
        per_device, mesh=mesh, in_specs=in_specs, out_specs=out_specs, check_vma=False
    )
```
